32 devices in a mesh: groups: 2 (over y), frame: 4 (over z), patch: 2 (over x), head: 2 (over core).
Axes of the slice: x: 2, y: 2, z: 4, core: 2. Of those that a mesh axis runs over, the one named last changes fastest.
Arguments:
- video: bfloat16 [16, 8, 1152], P(('groups', 'frame'), 'patch'), parts along dimension 0, may hold values from -1.5 to 1.5
- gain_time: float32 [1152], replicated, may hold values from 0.1 to 1.9
- qkv_time: bfloat16 [1152, 3, 1152], P('frame', None, 'head'), may hold values from -0.5343196 to 0.5343196
- out_time: bfloat16 [1152, 1152], P('frame', 'head'), may hold values from -0.1875 to 0.1875
- gain_space: float32 [1152], replicated, may hold values from 0.1 to 1.9
- qkv_space: bfloat16 [1152, 3, 1152], P('frame', None, 'head'), may hold values from -0.5343196 to 0.5343196
- out_space: bfloat16 [1152, 1152], P('frame', 'head'), may hold values from -0.1875 to 0.1875
Outputs:
- result: float32 [16, 8, 1152], P(('groups', 'frame', 'patch')), parts along dimension 0
The draws below stay inside these ranges and needn't reach their ends.
There are 2 independent parts, one for each index of `groups`. The reference program is written for one: setup_inputs(seed, part) draws one part's arguments, and reference() takes and returns one part's arrays. A program takes and returns all parts, laid end to end along the dimension named above; an argument that names none is the same for every part. Nothing has to cross between parts.
All inputs are finite; a program needn't handle non-finite values.
Results may differ from the reference program's by a relative error of at most 0.04.
Values may be sent and summed in bfloat16 or wider, within the bound.
A program may use at most 64 MiB of HBM per device.

```python
import jax
import jax.numpy as jnp
from jax import lax

D = 1152
HEADS = 16
HEAD_WIDTH = 72
FRAMES = 8
PATCHES = 8
N_HEAD = 2


def draw_video(key, part):
    value_rows = 0.25 * jnp.clip(jax.random.normal(jax.random.fold_in(key, 7), (FRAMES, PATCHES, D), jnp.float32), -6.0, 6.0)
    return value_rows.astype(jnp.bfloat16)


def drawn_weight(key):
    matrix_key = jax.random.fold_in(key, 1)
    matrix = jnp.clip(jax.random.normal(matrix_key, (D, 3, D), jnp.float32), -3.0, 3.0) * (1.0 / D ** 0.5)
    return matrix.astype(jnp.bfloat16)


def draw_qkv_time(key, part):
    return drawn_weight(jax.random.fold_in(key, 21))


def draw_qkv_space(key, part):
    return drawn_weight(jax.random.fold_in(key, 37))


def levels(key, extent, cuts, smallest, largest):
    def one(dim, parts):
        draws = jax.random.uniform(jax.random.fold_in(jax.random.fold_in(key, 6), dim), (parts,), jnp.float32, smallest / len(cuts), largest / len(cuts))
        return jnp.repeat(jnp.exp(draws), extent[dim] // parts).reshape((-1,) + (1,) * (len(extent) - dim - 1))

    factor_of = one(*cuts[0])
    for cut in cuts[1:]:
        factor_of = factor_of * one(*cut)
    return factor_of


def scatter_about(own_key, extent, scale, bound, pieces=(), kind=jnp.bfloat16):
    factor_of = levels(own_key, extent, pieces, -0.22, 0.18) if pieces else 1.0
    array = jax.random.normal(own_key, extent, jnp.float32) * scale * factor_of
    return jnp.minimum(jnp.maximum(array, -bound), bound).astype(kind)


def setup_inputs(seed: int = 0, part: int = 0) -> dict:
    key_of = jax.random.split(jax.random.key(seed), 8)
    part_keys = jax.random.split(jax.random.fold_in(key_of[7], part), 8)
    return {
        "video": draw_video(jax.random.fold_in(jax.random.fold_in(key_of[7], part), 71), part),
        "gain_time": jnp.clip(1.0 + 0.18 * jax.random.normal(key_of[1], (D,), jnp.float32), 0.1, 1.9),
        "qkv_time": draw_qkv_time(jax.random.fold_in(key_of[7], 71), part),
        "out_time": scatter_about(key_of[3], (D, D), D ** -0.5, 0.1875, ((0, 4), (1, 2))),
        "gain_space": jnp.clip(1.0 + 0.18 * jax.random.normal(key_of[4], (D,), jnp.float32), 0.1, 1.9),
        "qkv_space": draw_qkv_space(jax.random.fold_in(key_of[7], 71), part),
        "out_space": scatter_about(key_of[6], (D, D), D ** -0.5, 0.1875, ((0, 4), (1, 2))),
    }


def layer_norm(tokens, gain):
    value_rows = tokens.astype(jnp.float32)
    center = lax.optimization_barrier(jnp.mean(value_rows, axis=-1, keepdims=True))
    spread = lax.optimization_barrier(jnp.mean((value_rows - center) ** 2, axis=-1, keepdims=True))
    return ((value_rows - center) * lax.rsqrt(spread + 1e-06) * gain).astype(jnp.bfloat16)

def attend_one(packed):
    query_rows = packed[:, 0].astype(jnp.float32)
    key_rows = packed[:, 1].astype(jnp.float32)
    value_rows = packed[:, 2].astype(jnp.float32)
    score_matrix = jnp.einsum('pzo,ezo->zpe', query_rows, key_rows) / jnp.sqrt(jnp.float32(HEAD_WIDTH))
    attention_weights = jax.nn.softmax(score_matrix, axis=-1).astype(jnp.bfloat16).astype(jnp.float32)
    attention_output = jnp.einsum('jrc,cjn->rjn', attention_weights, value_rows).astype(jnp.bfloat16)
    return attention_output.reshape(attention_output.shape[0], -1)

def mix_block(tokens, gain, qkv_weight, out_weight, over_first):
    rows_a, rows_b, width = tokens.shape
    flat = tokens.reshape(rows_a * rows_b, width)
    normed = layer_norm(flat, gain)
    qkv = jnp.dot(normed, qkv_weight.reshape(width, 3 * width), preferred_element_type=jnp.float32)
    qkv = qkv.astype(jnp.bfloat16).reshape(rows_a, rows_b, 3, HEADS, HEAD_WIDTH)
    if over_first:
        batches = jnp.transpose(qkv, (1, 0, 2, 3, 4))
        attended = jnp.transpose(lax.map(attend_one, batches), (1, 0, 2))
    else:
        attended = lax.map(attend_one, qkv)
    attended = attended.reshape(rows_a * rows_b, width)
    share = width // N_HEAD
    total = jnp.zeros((rows_a * rows_b, width), jnp.float32)
    for group in range(N_HEAD):
        partial_value = jnp.dot(attended[:, group * share:(group + 1) * share], out_weight[:, group * share:(group + 1) * share].T, preferred_element_type=jnp.float32)
        total = total + lax.optimization_barrier(partial_value.astype(jnp.bfloat16)).astype(jnp.float32)
    return (flat.astype(jnp.float32) + total).reshape(rows_a, rows_b, width)

def reference(video, gain_time, qkv_time, out_time, gain_space, qkv_space, out_space):
    after_time = mix_block(video, gain_time, qkv_time, out_time, True).astype(jnp.bfloat16)
    return mix_block(after_time, gain_space, qkv_space, out_space, False)
```

```python
import functools

import jax
import jax.numpy as jnp
import numpy as np
from jax import lax
from jax.experimental import pallas as pl
from jax.experimental.pallas import tpu as pltpu
from jax.sharding import PartitionSpec as P

HEAD_WIDTH = 72


def layer_norm(tokens, gain):
    value_rows = tokens.astype(jnp.float32)
    center = jnp.mean(value_rows, axis=-1, keepdims=True)
    spread = jnp.mean((value_rows - center) ** 2, axis=-1, keepdims=True)
    return ((value_rows - center) * lax.rsqrt(spread + 1e-06) * gain).astype(jnp.bfloat16)


def project_qkv(normed, weight):
    columns = weight.shape[1] * weight.shape[2]
    total = jnp.dot(
        normed, weight.reshape(weight.shape[0], columns), preferred_element_type=jnp.float32
    )
    return total.astype(jnp.bfloat16)


def project_out(attended, weight):
    return lax.dot_general(
        attended, weight, (((1,), (1,)), ((), ())), preferred_element_type=jnp.float32
    )


def attend(qkv, over_first):
    query_rows, key_rows, value_rows = (qkv[:, :, 0], qkv[:, :, 1], qkv[:, :, 2])
    factor = 1.0 / jnp.sqrt(jnp.float32(HEAD_WIDTH))
    if over_first:
        score_matrix = (
            jnp.einsum("abhd,cbhd->bhac", query_rows, key_rows, preferred_element_type=jnp.float32)
            * factor
        )
        attention_weights = jax.nn.softmax(score_matrix, axis=-1).astype(jnp.bfloat16)
        attention_output = jnp.einsum(
            "bhac,cbhd->abhd", attention_weights, value_rows, preferred_element_type=jnp.float32
        )
    else:
        score_matrix = (
            jnp.einsum("abhd,achd->ahbc", query_rows, key_rows, preferred_element_type=jnp.float32)
            * factor
        )
        attention_weights = jax.nn.softmax(score_matrix, axis=-1).astype(jnp.bfloat16)
        attention_output = jnp.einsum(
            "ahbc,achd->abhd", attention_weights, value_rows, preferred_element_type=jnp.float32
        )
    return attention_output.astype(jnp.bfloat16)


def mix_partial(tokens, gain, qkv_weight, out_weight, over_first):
    rows_a, rows_b, width = tokens.shape
    flat = tokens.reshape(rows_a * rows_b, width)
    normed = layer_norm(flat, gain)
    qkv = project_qkv(normed, qkv_weight).reshape(rows_a, rows_b, 3, -1, HEAD_WIDTH)
    attended = attend(qkv, over_first).reshape(rows_a * rows_b, -1)
    partial_value = project_out(attended, out_weight)
    rounded = lax.optimization_barrier(partial_value.astype(jnp.bfloat16)).astype(jnp.float32)
    return (flat, rounded)


def on_device(video, gain_time, qkv_time, out_time, gain_space, qkv_space, out_space):
    frame_size = lax.axis_size("frame")
    patch_size = lax.axis_size("patch")
    device_count = frame_size * patch_size
    series = lax.all_to_all(video, "frame", split_axis=1, concat_axis=0, tiled=True)
    qkv_time, out_time, qkv_space, out_space = (
        lax.all_gather(qkv_time, "frame", axis=0, tiled=True),
        lax.all_gather(out_time, "frame", axis=0, tiled=True),
        lax.all_gather(qkv_space, "frame", axis=0, tiled=True),
        lax.all_gather(out_space, "frame", axis=0, tiled=True),
    )
    frame_count, series_count, width = series.shape
    set_count = frame_count // device_count
    flat, rounded = mix_partial(series, gain_time, qkv_time, out_time, True)
    summed = (
        lax.psum(rounded.astype(jnp.bfloat16), "head")
        .astype(jnp.float32)
        .reshape(device_count, set_count, series_count, width)
    )
    resident = flat.reshape(device_count, set_count, series_count, width)
    after_time = (resident.astype(jnp.float32) + summed).astype(jnp.bfloat16)
    arrived = lax.all_to_all(
        after_time, ("frame", "patch"), split_axis=0, concat_axis=2, tiled=True
    )
    whole_frames = arrived.reshape(set_count, device_count * series_count, width)
    whole_frames = whole_frames.reshape(set_count, frame_size, patch_size, series_count, width)
    whole_frames = jnp.transpose(whole_frames, (0, 2, 1, 3, 4)).reshape(
        set_count, device_count * series_count, width
    )
    flat_space, rounded_space = mix_partial(whole_frames, gain_space, qkv_space, out_space, False)
    summed_space = lax.psum(rounded_space.astype(jnp.bfloat16), "head").astype(jnp.float32)
    result = flat_space.astype(jnp.float32) + summed_space
    return result.reshape(whole_frames.shape)


MESH = pl.DeviceIdType.MESH
BF16 = jnp.bfloat16
F32 = jnp.float32


class Plan:
    def __init__(self, mesh_shape, video, qkv):
        self.frame_n = mesh_shape["frame"]
        self.patch_n = mesh_shape["patch"]
        self.head_n = mesh_shape["head"]
        self.frames, self.patches, self.width = video
        self.depth = qkv[0]
        self.cols = qkv[2]
        self.heads = self.cols // HEAD_WIDTH
        self.time_len = self.frames * self.frame_n
        self.space_len = self.patches * self.patch_n
        self.rows = self.time_len * self.patches
        self.own_rows = self.frames * self.patches
        self.series = self.patches // self.frame_n
        self.sets = self.frames // self.patch_n
        self.part_rows = self.rows // self.patch_n
        self.dest_rows = self.rows // self.frame_n

    def moves_less(self):
        divides = (
            self.patches % self.frame_n == 0
            and self.frames % self.patch_n == 0
            and self.dest_rows % 8 == 0
        )
        tokens = 2 * self.rows * (4 * self.cols + 2 * self.width)
        weights = 2 * (self.frame_n - 1) * self.depth * 4 * self.cols
        return divides and tokens < weights


def row_moves(plan):
    rows, frames, patches = plan.rows, plan.frames, plan.patches
    sources = plan.patch_n * rows
    both = plan.head_n * rows
    matrix = np.zeros((3 + plan.patch_n, rows, max(sources, both)), np.float32)
    for t in range(plan.time_len):
        for b in range(patches):
            matrix[0, b * plan.time_len + t, t * patches + b] = 1
    for f in range(plan.frame_n):
        for p in range(plan.patch_n):
            for s in range(plan.sets):
                for b in range(patches):
                    at = (f * plan.sets + s) * patches + b
                    row = p * plan.part_rows + at
                    frame = (f * plan.patch_n + p) * plan.sets + s
                    matrix[1, row, b * plan.time_len + frame] = 1
                    placed = ((f * plan.sets + s) * plan.patch_n + p) * patches + b
                    for h in range(plan.head_n):
                        matrix[2, placed, h * rows + row] = 1
                    for mine in range(plan.patch_n):
                        local = mine * plan.sets + s
                        source = ((p * plan.frame_n + f) * frames + local) * patches + b
                        matrix[3 + mine, placed, source] = 1
    return jnp.asarray(matrix, BF16)


def dot(a, b):
    return jnp.dot(a, b, preferred_element_type=F32)


def dot_t(a, b):
    return lax.dot_general(a, b, (((1,), (1,)), ((), ())), preferred_element_type=F32)


def attend_rows(query, key, value, length, heads):
    cols = query.shape[1]
    lane = lax.broadcasted_iota(jnp.int32, (length, cols), 1)
    masks = [(lane >= i * HEAD_WIDTH) & (lane < (i + 1) * HEAD_WIDTH) for i in range(heads)]
    factor = 1.0 / HEAD_WIDTH**0.5
    pieces = []
    for start in range(0, query.shape[0], length):
        q, k, v = (x[start : start + length] for x in (query, key, value))
        spread = jnp.concatenate([jnp.where(m, q, 0.0) for m in masks], axis=0).astype(BF16)
        score = dot_t(spread, k.astype(BF16)) * factor
        score = jnp.exp(score - jnp.max(score, axis=-1, keepdims=True))
        weight = (score / jnp.sum(score, axis=-1, keepdims=True)).astype(BF16)
        mixed = dot(weight, v.astype(BF16))
        total = jnp.zeros((length, cols), F32)
        for i, m in enumerate(masks):
            total = total + jnp.where(m, mixed[i * length : (i + 1) * length], 0.0)
        pieces.append(total)
    return jnp.concatenate(pieces, axis=0) if len(pieces) > 1 else pieces[0]


def normed_slice(slots, own, gain, width):
    center = sum(jnp.sum(s, axis=-1, keepdims=True) for s in slots) * (1.0 / width)
    spread = sum(jnp.sum((s - center) ** 2, axis=-1, keepdims=True) for s in slots) * (1.0 / width)
    return ((own - center) * lax.rsqrt(spread + 1e-06) * gain).astype(BF16)


def block_kernel(
    plan, video, gain_t, gain_s, moves, wq_t_hbm, wo_t_hbm, wq_s_hbm, wo_s_hbm, result,
    wq_t, wo_t, wq_s, wo_s, staged, gains, vid, base, after, part_t, got_t, part_s, got_s,
    att_t, att_s, proj, proj_all, last, last_all,
    w_sem, vid_sem, got_t_sem, got_s_sem, att_t_sem, att_s_sem, proj_sem, last_sem,
):
    g, f, p, h = (lax.axis_index(a) for a in ("groups", "frame", "patch", "head"))
    fn, pn, hn, depth = plan.frame_n, plan.patch_n, plan.head_n, plan.depth

    def place(df, dp, dh):
        return (g, lax.rem(f + df, fn), lax.rem(p + dp, pn), lax.rem(h + dh, hn))

    loads = [
        pltpu.make_async_copy(src, dst, w_sem.at[i])
        for i, (src, dst) in enumerate(
            ((wq_t_hbm, wq_t), (wo_t_hbm, wo_t), (wq_s_hbm, wq_s), (wo_s_hbm, wo_s))
        )
    ]
    for load in loads:
        load.start()

    barrier = pltpu.get_barrier_semaphore()
    offsets = [
        (df, dp, dh) for df in range(fn) for dp in range(pn) for dh in range(hn) if df + dp + dh
    ]
    for offset in offsets:
        pl.semaphore_signal(barrier, inc=1, device_id=place(*offset), device_id_type=MESH)

    for i in range(plan.frames):
        staged[i * plan.patches : (i + 1) * plan.patches] = video[i].astype(F32)
    for j in range(fn):
        lanes = slice(j * depth, (j + 1) * depth)
        vid[p, f, j] = staged[:, lanes].astype(BF16)
        gains[0, j] = gain_t[:, lanes]
        gains[1, j] = gain_s[:, lanes]
    pl.semaphore_wait(barrier, len(offsets))

    sent = []

    def push(src, dst, sems, number, target):
        copy = pltpu.make_async_remote_copy(
            src_ref=src, dst_ref=dst, send_sem=sems.at[0, number], recv_sem=sems.at[1, number],
            device_id=target, device_id_type=MESH,
        )
        copy.start()
        sent.append(copy)
        return copy

    near = [
        push(vid.at[p, f], vid.at[p, f], vid_sem, df, place(df, 0, 0)) for df in range(1, fn)
    ]
    far = [
        push(vid.at[p, f], vid.at[p, f], vid_sem, dp * fn + df, place(df, dp, 0))
        for dp in range(1, pn)
        for df in range(fn)
    ]

    def spread_attention(normed, wq, part, got, got_sem, att, att_sem, length):
        for kind in range(3):
            product = dot(normed, wq[kind])
            for j in range(fn):
                piece = product[j * plan.dest_rows : (j + 1) * plan.dest_rows]
                part[j, kind] = piece.astype(BF16)
        copies = [
            push(part.at[lax.rem(f + df, fn)], got.at[df - 1], got_sem, df, place(df, 0, 0))
            for df in range(1, fn)
        ]
        total = [part[f, kind].astype(F32) for kind in range(3)]
        for df, copy in enumerate(copies):
            copy.wait_recv()
            total = [total[kind] + got[df, kind].astype(F32) for kind in range(3)]
        total = [t.astype(BF16).astype(F32) for t in total]
        att[f] = attend_rows(*total, length, plan.heads).astype(BF16)
        copies = [
            push(att.at[f], att.at[f], att_sem, df, place(df, 0, 0)) for df in range(1, fn)
        ]
        for copy in copies:
            copy.wait_recv()
        return jnp.concatenate([att[j].astype(F32) for j in range(fn)], axis=0).astype(BF16)

    for copy in near:
        copy.wait_recv()

    def series_slot(j):
        return jnp.concatenate([vid[p, s, j].astype(F32) for s in range(fn)], axis=0)

    normed = normed_slice(
        [series_slot(j) for j in range(fn)], series_slot(f), gains[0, f], plan.width
    )
    normed = dot(moves[0][:, : plan.rows], normed).astype(BF16)
    loads[0].wait()
    attended = spread_attention(
        normed, wq_t, part_t, got_t, got_t_sem, att_t, att_t_sem, plan.time_len
    )
    loads[1].wait()
    partial_value = dot_t(attended, wo_t[...]).astype(BF16)
    partial_value = dot(moves[1][:, : plan.rows], partial_value).astype(BF16)
    for q in range(pn):
        proj[q] = partial_value[q * plan.part_rows : (q + 1) * plan.part_rows]
    copies = []
    for number, offset in enumerate(offsets):
        target = place(*offset)
        copies.append(push(proj.at[target[2]], proj_all.at[h, p, f], proj_sem, number, target))
    proj_all[h, p, f] = proj[p]

    for copy in far:
        copy.wait_recv()
    for j in range(fn):
        stacked = jnp.concatenate(
            [vid[q, s, j].astype(F32) for q in range(pn) for s in range(fn)], axis=0
        )
        base[j] = dot(moves[3 + p][:, : pn * plan.rows], stacked.astype(BF16))
    for copy in copies:
        copy.wait_recv()
    slots = []
    for j in range(fn):
        stacked = jnp.concatenate(
            [proj_all[k, q, j].astype(F32) for k in range(hn) for q in range(pn)], axis=0
        )
        added = base[j] + dot(moves[2][:, : hn * plan.rows], stacked.astype(BF16))
        slot = added.astype(BF16).astype(F32)
        for s in range(fn):
            after[j, s] = slot[s * plan.dest_rows : (s + 1) * plan.dest_rows]
        slots.append(slot)
    own = jnp.concatenate([after[f, s] for s in range(fn)], axis=0)
    normed = normed_slice(slots, own, gains[1, f], plan.width)
    loads[2].wait()
    attended = spread_attention(
        normed, wq_s, part_s, got_s, got_s_sem, att_s, att_s_sem, plan.space_len
    )
    loads[3].wait()
    partial_value = dot_t(attended, wo_s[...])
    for j in range(fn):
        last[j] = partial_value[j * plan.dest_rows : (j + 1) * plan.dest_rows].astype(BF16)
    copies = []
    for dh in range(hn):
        for df in range(fn):
            if df + dh:
                target = place(df, 0, dh)
                number = dh * fn + df
                copies.append(push(last.at[target[1]], last_all.at[h, f], last_sem, number, target))
    last_all[h, f] = last[f]
    for copy in copies:
        copy.wait_recv()
    for j in range(fn):
        total = after[j, f]
        for k in range(hn):
            total = total + last_all[k, j].astype(F32)
        result[:, j * depth : (j + 1) * depth] = total
    for copy in sent:
        copy.wait_send()


def move_tokens(plan, video, gain_time, qkv_time, out_time, gain_space, qkv_space, out_space):
    fn, pn, hn, depth, cols = plan.frame_n, plan.patch_n, plan.head_n, plan.depth, plan.cols
    own, dest, rows = plan.own_rows, plan.dest_rows, plan.rows
    vmem = pl.BlockSpec(memory_space=pltpu.VMEM)
    hbm = pl.BlockSpec(memory_space=pl.ANY)
    everyone = fn * pn * hn
    pairs = lambda count: pltpu.SemaphoreType.DMA((2, count))
    result = pl.pallas_call(
        functools.partial(block_kernel, plan),
        out_shape=jax.ShapeDtypeStruct((plan.sets * plan.space_len, plan.width), F32),
        in_specs=[vmem] * 4 + [hbm] * 4,
        out_specs=vmem,
        scratch_shapes=[
            pltpu.VMEM((3, depth, cols), BF16),
            pltpu.VMEM((depth, cols), BF16),
            pltpu.VMEM((3, depth, cols), BF16),
            pltpu.VMEM((depth, cols), BF16),
            pltpu.VMEM((own, plan.width), F32),
            pltpu.VMEM((2, fn, 1, depth), F32),
            pltpu.VMEM((pn, fn, fn, own, depth), BF16),
            pltpu.VMEM((fn, rows, depth), F32),
            pltpu.VMEM((fn, fn, dest, depth), F32),
            pltpu.VMEM((fn, 3, dest, cols), BF16),
            pltpu.VMEM((max(fn - 1, 1), 3, dest, cols), BF16),
            pltpu.VMEM((fn, 3, dest, cols), BF16),
            pltpu.VMEM((max(fn - 1, 1), 3, dest, cols), BF16),
            pltpu.VMEM((fn, dest, cols), BF16),
            pltpu.VMEM((fn, dest, cols), BF16),
            pltpu.VMEM((pn, plan.part_rows, depth), BF16),
            pltpu.VMEM((hn, pn, fn, plan.part_rows, depth), BF16),
            pltpu.VMEM((fn, dest, depth), BF16),
            pltpu.VMEM((hn, fn, dest, depth), BF16),
            pltpu.SemaphoreType.DMA((4,)),
            pairs(pn * fn),
            pairs(fn),
            pairs(fn),
            pairs(fn),
            pairs(fn),
            pairs(everyone),
            pairs(hn * fn),
        ],
        compiler_params=pltpu.CompilerParams(
            collective_id=0, has_side_effects=True, vmem_limit_bytes=48 * 1024 * 1024
        ),
    )(
        video,
        gain_time.reshape(1, -1),
        gain_space.reshape(1, -1),
        row_moves(plan),
        jnp.transpose(qkv_time, (1, 0, 2)),
        out_time,
        jnp.transpose(qkv_space, (1, 0, 2)),
        out_space,
    )
    return result.reshape(plan.sets, plan.space_len, plan.width)


def solution(mesh):
    placed = (
        P(("groups", "frame"), "patch", None),
        P(),
        P("frame", None, "head"),
        P("frame", "head"),
        P(),
        P("frame", None, "head"),
        P("frame", "head"),
    )

    def on_one(video, gain_time, qkv_time, *others):
        plan = Plan(mesh.shape, video.shape, qkv_time.shape)
        if plan.moves_less():
            return move_tokens(plan, video, gain_time, qkv_time, *others)
        return on_device(video, gain_time, qkv_time, *others)

    return jax.shard_map(
        on_one,
        mesh=mesh,
        in_specs=placed,
        out_specs=P(("groups", "frame", "patch"), None, None),
        check_vma=False,
    )
```

```python
import functools

import jax
import jax.numpy as jnp
import numpy as np
from jax import lax
from jax.experimental import pallas as pl
from jax.experimental.pallas import tpu as pltpu
from jax.sharding import PartitionSpec as P

HEAD_WIDTH = 72


def layer_norm(tokens, gain):
    value_rows = tokens.astype(jnp.float32)
    center = jnp.mean(value_rows, axis=-1, keepdims=True)
    spread = jnp.mean((value_rows - center) ** 2, axis=-1, keepdims=True)
    return ((value_rows - center) * lax.rsqrt(spread + 1e-06) * gain).astype(jnp.bfloat16)


def project_qkv(normed, weight):
    columns = weight.shape[1] * weight.shape[2]
    total = jnp.dot(
        normed, weight.reshape(weight.shape[0], columns), preferred_element_type=jnp.float32
    )
    return total.astype(jnp.bfloat16)


def project_out(attended, weight):
    return lax.dot_general(
        attended, weight, (((1,), (1,)), ((), ())), preferred_element_type=jnp.float32
    )


def attend(qkv, over_first):
    query_rows, key_rows, value_rows = (qkv[:, :, 0], qkv[:, :, 1], qkv[:, :, 2])
    factor = 1.0 / jnp.sqrt(jnp.float32(HEAD_WIDTH))
    if over_first:
        score_matrix = (
            jnp.einsum("abhd,cbhd->bhac", query_rows, key_rows, preferred_element_type=jnp.float32)
            * factor
        )
        attention_weights = jax.nn.softmax(score_matrix, axis=-1).astype(jnp.bfloat16)
        attention_output = jnp.einsum(
            "bhac,cbhd->abhd", attention_weights, value_rows, preferred_element_type=jnp.float32
        )
    else:
        score_matrix = (
            jnp.einsum("abhd,achd->ahbc", query_rows, key_rows, preferred_element_type=jnp.float32)
            * factor
        )
        attention_weights = jax.nn.softmax(score_matrix, axis=-1).astype(jnp.bfloat16)
        attention_output = jnp.einsum(
            "ahbc,achd->abhd", attention_weights, value_rows, preferred_element_type=jnp.float32
        )
    return attention_output.astype(jnp.bfloat16)


def mix_partial(tokens, gain, qkv_weight, out_weight, over_first):
    rows_a, rows_b, width = tokens.shape
    flat = tokens.reshape(rows_a * rows_b, width)
    normed = layer_norm(flat, gain)
    qkv = project_qkv(normed, qkv_weight).reshape(rows_a, rows_b, 3, -1, HEAD_WIDTH)
    attended = attend(qkv, over_first).reshape(rows_a * rows_b, -1)
    partial_value = project_out(attended, out_weight)
    rounded = lax.optimization_barrier(partial_value.astype(jnp.bfloat16)).astype(jnp.float32)
    return (flat, rounded)


def on_device(video, gain_time, qkv_time, out_time, gain_space, qkv_space, out_space):
    frame_size = lax.axis_size("frame")
    patch_size = lax.axis_size("patch")
    device_count = frame_size * patch_size
    series = lax.all_to_all(video, "frame", split_axis=1, concat_axis=0, tiled=True)
    qkv_time, out_time, qkv_space, out_space = (
        lax.all_gather(qkv_time, "frame", axis=0, tiled=True),
        lax.all_gather(out_time, "frame", axis=0, tiled=True),
        lax.all_gather(qkv_space, "frame", axis=0, tiled=True),
        lax.all_gather(out_space, "frame", axis=0, tiled=True),
    )
    frame_count, series_count, width = series.shape
    set_count = frame_count // device_count
    flat, rounded = mix_partial(series, gain_time, qkv_time, out_time, True)
    summed = (
        lax.psum(rounded.astype(jnp.bfloat16), "head")
        .astype(jnp.float32)
        .reshape(device_count, set_count, series_count, width)
    )
    resident = flat.reshape(device_count, set_count, series_count, width)
    after_time = (resident.astype(jnp.float32) + summed).astype(jnp.bfloat16)
    arrived = lax.all_to_all(
        after_time, ("frame", "patch"), split_axis=0, concat_axis=2, tiled=True
    )
    whole_frames = arrived.reshape(set_count, device_count * series_count, width)
    whole_frames = whole_frames.reshape(set_count, frame_size, patch_size, series_count, width)
    whole_frames = jnp.transpose(whole_frames, (0, 2, 1, 3, 4)).reshape(
        set_count, device_count * series_count, width
    )
    flat_space, rounded_space = mix_partial(whole_frames, gain_space, qkv_space, out_space, False)
    summed_space = lax.psum(rounded_space.astype(jnp.bfloat16), "head").astype(jnp.float32)
    result = flat_space.astype(jnp.float32) + summed_space
    return result.reshape(whole_frames.shape)


MESH = pl.DeviceIdType.MESH
BF16 = jnp.bfloat16
F32 = jnp.float32


class Plan:
    def __init__(self, mesh_shape, video, qkv):
        self.frame_n = mesh_shape["frame"]
        self.patch_n = mesh_shape["patch"]
        self.head_n = mesh_shape["head"]
        self.frames, self.patches, self.width = video
        self.depth = qkv[0]
        self.cols = qkv[2]
        self.heads = self.cols // HEAD_WIDTH
        self.time_len = self.frames * self.frame_n
        self.space_len = self.patches * self.patch_n
        self.rows = self.time_len * self.patches
        self.own_rows = self.frames * self.patches
        self.series = self.patches // self.frame_n
        self.sets = self.frames // self.patch_n
        self.part_rows = self.rows // self.patch_n
        self.dest_rows = self.rows // self.frame_n

    def moves_less(self):
        divides = (
            self.patches % self.frame_n == 0
            and self.frames % self.patch_n == 0
            and self.dest_rows % 8 == 0
        )
        tokens = 2 * self.rows * (4 * self.cols + 2 * self.width)
        weights = 2 * (self.frame_n - 1) * self.depth * 4 * self.cols
        return divides and tokens < weights


def row_moves(plan):
    rows, frames, patches = plan.rows, plan.frames, plan.patches
    sources = plan.patch_n * rows
    both = plan.head_n * rows
    matrix = np.zeros((3 + plan.patch_n, rows, max(sources, both)), np.float32)
    for t in range(plan.time_len):
        for b in range(patches):
            matrix[0, b * plan.time_len + t, t * patches + b] = 1
    for f in range(plan.frame_n):
        for p in range(plan.patch_n):
            for s in range(plan.sets):
                for b in range(patches):
                    at = (f * plan.sets + s) * patches + b
                    row = p * plan.part_rows + at
                    frame = (f * plan.patch_n + p) * plan.sets + s
                    matrix[1, row, b * plan.time_len + frame] = 1
                    placed = ((f * plan.sets + s) * plan.patch_n + p) * patches + b
                    for h in range(plan.head_n):
                        matrix[2, placed, h * rows + row] = 1
                    for mine in range(plan.patch_n):
                        local = mine * plan.sets + s
                        source = ((p * plan.frame_n + f) * frames + local) * patches + b
                        matrix[3 + mine, placed, source] = 1
    return jnp.asarray(matrix, BF16)


def dot(a, b):
    return jnp.dot(a, b, preferred_element_type=F32)


def dot_t(a, b):
    return lax.dot_general(a, b, (((1,), (1,)), ((), ())), preferred_element_type=F32)


def attend_rows(query, key, value, length, heads):
    cols = query.shape[1]
    lane = lax.broadcasted_iota(jnp.int32, (length, cols), 1)
    masks = [(lane >= i * HEAD_WIDTH) & (lane < (i + 1) * HEAD_WIDTH) for i in range(heads)]
    factor = 1.0 / HEAD_WIDTH**0.5
    pieces = []
    for start in range(0, query.shape[0], length):
        q, k, v = (x[start : start + length] for x in (query, key, value))
        spread = jnp.concatenate([jnp.where(m, q, 0.0) for m in masks], axis=0).astype(BF16)
        score = dot_t(spread, k.astype(BF16)) * factor
        score = jnp.exp(score - jnp.max(score, axis=-1, keepdims=True))
        weight = (score / jnp.sum(score, axis=-1, keepdims=True)).astype(BF16)
        mixed = dot(weight, v.astype(BF16))
        total = jnp.zeros((length, cols), F32)
        for i, m in enumerate(masks):
            total = total + jnp.where(m, mixed[i * length : (i + 1) * length], 0.0)
        pieces.append(total)
    return jnp.concatenate(pieces, axis=0) if len(pieces) > 1 else pieces[0]


def normed_slice(slots, own, gain, width):
    center = sum(jnp.sum(s, axis=-1, keepdims=True) for s in slots) * (1.0 / width)
    spread = sum(jnp.sum((s - center) ** 2, axis=-1, keepdims=True) for s in slots) * (1.0 / width)
    return ((own - center) * lax.rsqrt(spread + 1e-06) * gain).astype(BF16)


def block_kernel(
    plan, video_hbm, gain_t_hbm, gain_s_hbm, moves_hbm, wq_t_hbm, wo_t_hbm, wq_s_hbm, wo_s_hbm,
    result, video, gain_t, gain_s, moves, wq_t, wo_t, wq_s, wo_s, staged, gains, vid, base, after, part_t, got_t, part_s, got_s,
    att_t, att_s, proj, proj_all, last, last_all,
    w_sem, vid_sem, got_t_sem, got_s_sem, att_t_sem, att_s_sem, proj_sem, last_sem,
):
    g, f, p, h = (lax.axis_index(a) for a in ("groups", "frame", "patch", "head"))
    fn, pn, hn, depth = plan.frame_n, plan.patch_n, plan.head_n, plan.depth

    def place(df, dp, dh):
        return (g, lax.rem(f + df, fn), lax.rem(p + dp, pn), lax.rem(h + dh, hn))

    loads = [
        pltpu.make_async_copy(src, dst, w_sem.at[i])
        for i, (src, dst) in enumerate(
            (
                (wq_t_hbm, wq_t), (wo_t_hbm, wo_t), (wq_s_hbm, wq_s), (wo_s_hbm, wo_s),
                (video_hbm, video), (gain_t_hbm, gain_t), (gain_s_hbm, gain_s), (moves_hbm, moves),
            )
        )
    ]
    for load in loads[4:] + loads[:4]:
        load.start()

    barrier = pltpu.get_barrier_semaphore()
    offsets = [
        (df, dp, dh) for df in range(fn) for dp in range(pn) for dh in range(hn) if df + dp + dh
    ]
    for offset in offsets:
        pl.semaphore_signal(barrier, inc=1, device_id=place(*offset), device_id_type=MESH)

    loads[4].wait()
    for i in range(plan.frames):
        staged[i * plan.patches : (i + 1) * plan.patches] = video[i].astype(F32)
    for j in range(fn):
        lanes = slice(j * depth, (j + 1) * depth)
        vid[p, f, j] = staged[:, lanes].astype(BF16)
    pl.semaphore_wait(barrier, len(offsets))

    sent = []

    def push(src, dst, sems, number, target):
        copy = pltpu.make_async_remote_copy(
            src_ref=src, dst_ref=dst, send_sem=sems.at[0, number], recv_sem=sems.at[1, number],
            device_id=target, device_id_type=MESH,
        )
        copy.start()
        sent.append(copy)
        return copy

    near = [
        push(vid.at[p, f], vid.at[p, f], vid_sem, df, place(df, 0, 0)) for df in range(1, fn)
    ]
    far = [
        push(vid.at[p, f], vid.at[p, f], vid_sem, dp * fn + df, place(df, dp, 0))
        for dp in range(1, pn)
        for df in range(fn)
    ]

    for load in loads[5:]:
        load.wait()
    for j in range(fn):
        lanes = slice(j * depth, (j + 1) * depth)
        gains[0, j] = gain_t[...].reshape(1, plan.width)[:, lanes]
        gains[1, j] = gain_s[...].reshape(1, plan.width)[:, lanes]

    def spread_attention(normed, wq, part, got, got_sem, att, att_sem, length):
        for kind in range(3):
            product = dot(normed, wq[kind])
            for j in range(fn):
                piece = product[j * plan.dest_rows : (j + 1) * plan.dest_rows]
                part[j, kind] = piece.astype(BF16)
        copies = [
            push(part.at[lax.rem(f + df, fn)], got.at[df - 1], got_sem, df, place(df, 0, 0))
            for df in range(1, fn)
        ]
        total = [part[f, kind].astype(F32) for kind in range(3)]
        for df, copy in enumerate(copies):
            copy.wait_recv()
            total = [total[kind] + got[df, kind].astype(F32) for kind in range(3)]
        total = [t.astype(BF16).astype(F32) for t in total]
        att[f] = attend_rows(*total, length, plan.heads).astype(BF16)
        copies = [
            push(att.at[f], att.at[f], att_sem, df, place(df, 0, 0)) for df in range(1, fn)
        ]
        for copy in copies:
            copy.wait_recv()
        return jnp.concatenate([att[j].astype(F32) for j in range(fn)], axis=0).astype(BF16)

    for copy in near:
        copy.wait_recv()

    def series_slot(j):
        return jnp.concatenate([vid[p, s, j].astype(F32) for s in range(fn)], axis=0)

    normed = normed_slice(
        [series_slot(j) for j in range(fn)], series_slot(f), gains[0, f], plan.width
    )
    normed = dot(moves[0][:, : plan.rows], normed).astype(BF16)
    loads[0].wait()
    attended = spread_attention(
        normed, wq_t, part_t, got_t, got_t_sem, att_t, att_t_sem, plan.time_len
    )
    loads[1].wait()
    partial_value = dot_t(attended, wo_t[...]).astype(BF16)
    partial_value = dot(moves[1][:, : plan.rows], partial_value).astype(BF16)
    for q in range(pn):
        proj[q] = partial_value[q * plan.part_rows : (q + 1) * plan.part_rows]
    copies = []
    for number, offset in enumerate(offsets):
        target = place(*offset)
        copies.append(push(proj.at[target[2]], proj_all.at[h, p, f], proj_sem, number, target))
    proj_all[h, p, f] = proj[p]

    for copy in far:
        copy.wait_recv()
    for j in range(fn):
        stacked = jnp.concatenate(
            [vid[q, s, j].astype(F32) for q in range(pn) for s in range(fn)], axis=0
        )
        base[j] = dot(moves[3 + p][:, : pn * plan.rows], stacked.astype(BF16))
    for copy in copies:
        copy.wait_recv()
    slots = []
    for j in range(fn):
        stacked = jnp.concatenate(
            [proj_all[k, q, j].astype(F32) for k in range(hn) for q in range(pn)], axis=0
        )
        added = base[j] + dot(moves[2][:, : hn * plan.rows], stacked.astype(BF16))
        slot = added.astype(BF16).astype(F32)
        for s in range(fn):
            after[j, s] = slot[s * plan.dest_rows : (s + 1) * plan.dest_rows]
        slots.append(slot)
    own = jnp.concatenate([after[f, s] for s in range(fn)], axis=0)
    normed = normed_slice(slots, own, gains[1, f], plan.width)
    loads[2].wait()
    attended = spread_attention(
        normed, wq_s, part_s, got_s, got_s_sem, att_s, att_s_sem, plan.space_len
    )
    loads[3].wait()
    partial_value = dot_t(attended, wo_s[...])
    for j in range(fn):
        last[j] = partial_value[j * plan.dest_rows : (j + 1) * plan.dest_rows].astype(BF16)
    copies = []
    for dh in range(hn):
        for df in range(fn):
            if df + dh:
                target = place(df, 0, dh)
                number = dh * fn + df
                copies.append(push(last.at[target[1]], last_all.at[h, f], last_sem, number, target))
    last_all[h, f] = last[f]
    for copy in copies:
        copy.wait_recv()
    for j in range(fn):
        total = after[j, f]
        for k in range(hn):
            total = total + last_all[k, j].astype(F32)
        result[:, j * depth : (j + 1) * depth] = total
    for copy in sent:
        copy.wait_send()


def move_tokens(plan, video, gain_time, qkv_time, out_time, gain_space, qkv_space, out_space):
    fn, pn, hn, depth, cols = plan.frame_n, plan.patch_n, plan.head_n, plan.depth, plan.cols
    own, dest, rows = plan.own_rows, plan.dest_rows, plan.rows
    vmem = pl.BlockSpec(memory_space=pltpu.VMEM)
    hbm = pl.BlockSpec(memory_space=pltpu.HBM)
    everyone = fn * pn * hn
    moves = row_moves(plan)
    pairs = lambda count: pltpu.SemaphoreType.DMA((2, count))
    result = pl.pallas_call(
        functools.partial(block_kernel, plan),
        out_shape=jax.ShapeDtypeStruct((plan.sets * plan.space_len, plan.width), F32),
        in_specs=[hbm] * 8,
        out_specs=vmem,
        scratch_shapes=[
            pltpu.VMEM(video.shape, BF16),
            pltpu.VMEM(gain_time.shape, F32),
            pltpu.VMEM(gain_space.shape, F32),
            pltpu.VMEM(moves.shape, BF16),
            pltpu.VMEM((3, depth, cols), BF16),
            pltpu.VMEM((depth, cols), BF16),
            pltpu.VMEM((3, depth, cols), BF16),
            pltpu.VMEM((depth, cols), BF16),
            pltpu.VMEM((own, plan.width), F32),
            pltpu.VMEM((2, fn, 1, depth), F32),
            pltpu.VMEM((pn, fn, fn, own, depth), BF16),
            pltpu.VMEM((fn, rows, depth), F32),
            pltpu.VMEM((fn, fn, dest, depth), F32),
            pltpu.VMEM((fn, 3, dest, cols), BF16),
            pltpu.VMEM((max(fn - 1, 1), 3, dest, cols), BF16),
            pltpu.VMEM((fn, 3, dest, cols), BF16),
            pltpu.VMEM((max(fn - 1, 1), 3, dest, cols), BF16),
            pltpu.VMEM((fn, dest, cols), BF16),
            pltpu.VMEM((fn, dest, cols), BF16),
            pltpu.VMEM((pn, plan.part_rows, depth), BF16),
            pltpu.VMEM((hn, pn, fn, plan.part_rows, depth), BF16),
            pltpu.VMEM((fn, dest, depth), BF16),
            pltpu.VMEM((hn, fn, dest, depth), BF16),
            pltpu.SemaphoreType.DMA((8,)),
            pairs(pn * fn),
            pairs(fn),
            pairs(fn),
            pairs(fn),
            pairs(fn),
            pairs(everyone),
            pairs(hn * fn),
        ],
        compiler_params=pltpu.CompilerParams(
            collective_id=0, has_side_effects=True, vmem_limit_bytes=63 * 1024 * 1024
        ),
    )(
        video,
        gain_time,
        gain_space,
        moves,
        jnp.transpose(qkv_time, (1, 0, 2)),
        out_time,
        jnp.transpose(qkv_space, (1, 0, 2)),
        out_space,
    )
    return result.reshape(plan.sets, plan.space_len, plan.width)


def solution(mesh):
    placed = (
        P(("groups", "frame"), "patch", None),
        P(),
        P("frame", None, "head"),
        P("frame", "head"),
        P(),
        P("frame", None, "head"),
        P("frame", "head"),
    )

    def on_one(video, gain_time, qkv_time, *others):
        plan = Plan(mesh.shape, video.shape, qkv_time.shape)
        if plan.moves_less():
            return move_tokens(plan, video, gain_time, qkv_time, *others)
        return on_device(video, gain_time, qkv_time, *others)

    return jax.shard_map(
        on_one,
        mesh=mesh,
        in_specs=placed,
        out_specs=P(("groups", "frame", "patch"), None, None),
        check_vma=False,
    )
```

```python
import functools

import jax
import jax.numpy as jnp
import numpy as np
from jax import lax
from jax.experimental import pallas as pl
from jax.experimental.pallas import tpu as pltpu
from jax.sharding import PartitionSpec as P

HEAD_WIDTH = 72


def layer_norm(tokens, gain):
    value_rows = tokens.astype(jnp.float32)
    center = jnp.mean(value_rows, axis=-1, keepdims=True)
    spread = jnp.mean((value_rows - center) ** 2, axis=-1, keepdims=True)
    return ((value_rows - center) * lax.rsqrt(spread + 1e-06) * gain).astype(jnp.bfloat16)


def project_qkv(normed, weight):
    columns = weight.shape[1] * weight.shape[2]
    total = jnp.dot(
        normed, weight.reshape(weight.shape[0], columns), preferred_element_type=jnp.float32
    )
    return total.astype(jnp.bfloat16)


def project_out(attended, weight):
    return lax.dot_general(
        attended, weight, (((1,), (1,)), ((), ())), preferred_element_type=jnp.float32
    )


def attend(qkv, over_first):
    query_rows, key_rows, value_rows = (qkv[:, :, 0], qkv[:, :, 1], qkv[:, :, 2])
    factor = 1.0 / jnp.sqrt(jnp.float32(HEAD_WIDTH))
    if over_first:
        score_matrix = (
            jnp.einsum("abhd,cbhd->bhac", query_rows, key_rows, preferred_element_type=jnp.float32)
            * factor
        )
        attention_weights = jax.nn.softmax(score_matrix, axis=-1).astype(jnp.bfloat16)
        attention_output = jnp.einsum(
            "bhac,cbhd->abhd", attention_weights, value_rows, preferred_element_type=jnp.float32
        )
    else:
        score_matrix = (
            jnp.einsum("abhd,achd->ahbc", query_rows, key_rows, preferred_element_type=jnp.float32)
            * factor
        )
        attention_weights = jax.nn.softmax(score_matrix, axis=-1).astype(jnp.bfloat16)
        attention_output = jnp.einsum(
            "ahbc,achd->abhd", attention_weights, value_rows, preferred_element_type=jnp.float32
        )
    return attention_output.astype(jnp.bfloat16)


def mix_partial(tokens, gain, qkv_weight, out_weight, over_first):
    rows_a, rows_b, width = tokens.shape
    flat = tokens.reshape(rows_a * rows_b, width)
    normed = layer_norm(flat, gain)
    qkv = project_qkv(normed, qkv_weight).reshape(rows_a, rows_b, 3, -1, HEAD_WIDTH)
    attended = attend(qkv, over_first).reshape(rows_a * rows_b, -1)
    partial_value = project_out(attended, out_weight)
    rounded = lax.optimization_barrier(partial_value.astype(jnp.bfloat16)).astype(jnp.float32)
    return (flat, rounded)


def on_device(video, gain_time, qkv_time, out_time, gain_space, qkv_space, out_space):
    frame_size = lax.axis_size("frame")
    patch_size = lax.axis_size("patch")
    device_count = frame_size * patch_size
    series = lax.all_to_all(video, "frame", split_axis=1, concat_axis=0, tiled=True)
    qkv_time, out_time, qkv_space, out_space = (
        lax.all_gather(qkv_time, "frame", axis=0, tiled=True),
        lax.all_gather(out_time, "frame", axis=0, tiled=True),
        lax.all_gather(qkv_space, "frame", axis=0, tiled=True),
        lax.all_gather(out_space, "frame", axis=0, tiled=True),
    )
    frame_count, series_count, width = series.shape
    set_count = frame_count // device_count
    flat, rounded = mix_partial(series, gain_time, qkv_time, out_time, True)
    summed = (
        lax.psum(rounded.astype(jnp.bfloat16), "head")
        .astype(jnp.float32)
        .reshape(device_count, set_count, series_count, width)
    )
    resident = flat.reshape(device_count, set_count, series_count, width)
    after_time = (resident.astype(jnp.float32) + summed).astype(jnp.bfloat16)
    arrived = lax.all_to_all(
        after_time, ("frame", "patch"), split_axis=0, concat_axis=2, tiled=True
    )
    whole_frames = arrived.reshape(set_count, device_count * series_count, width)
    whole_frames = whole_frames.reshape(set_count, frame_size, patch_size, series_count, width)
    whole_frames = jnp.transpose(whole_frames, (0, 2, 1, 3, 4)).reshape(
        set_count, device_count * series_count, width
    )
    flat_space, rounded_space = mix_partial(whole_frames, gain_space, qkv_space, out_space, False)
    summed_space = lax.psum(rounded_space.astype(jnp.bfloat16), "head").astype(jnp.float32)
    result = flat_space.astype(jnp.float32) + summed_space
    return result.reshape(whole_frames.shape)


MESH = pl.DeviceIdType.MESH
BF16 = jnp.bfloat16
F32 = jnp.float32


class Plan:
    def __init__(self, mesh_shape, video, qkv):
        self.frame_n = mesh_shape["frame"]
        self.patch_n = mesh_shape["patch"]
        self.head_n = mesh_shape["head"]
        self.frames, self.patches, self.width = video
        self.depth = qkv[0]
        self.cols = qkv[2]
        self.heads = self.cols // HEAD_WIDTH
        self.time_len = self.frames * self.frame_n
        self.space_len = self.patches * self.patch_n
        self.rows = self.time_len * self.patches
        self.own_rows = self.frames * self.patches
        self.series = self.patches // self.frame_n
        self.sets = self.frames // self.patch_n
        self.part_rows = self.rows // self.patch_n
        self.dest_rows = self.rows // self.frame_n

    def moves_less(self):
        divides = (
            self.patches % self.frame_n == 0
            and self.frames % self.patch_n == 0
            and self.dest_rows % 8 == 0
        )
        tokens = 2 * self.rows * (4 * self.cols + 2 * self.width)
        weights = 2 * (self.frame_n - 1) * self.depth * 4 * self.cols
        return divides and tokens < weights


def row_moves(plan):
    rows, patches = plan.rows, plan.patches
    matrix = np.zeros((3, rows, rows), np.float32)
    for t in range(plan.time_len):
        for b in range(patches):
            matrix[0, b * plan.time_len + t, t * patches + b] = 1
    for f in range(plan.frame_n):
        for p in range(plan.patch_n):
            for s in range(plan.sets):
                for b in range(patches):
                    at = (f * plan.sets + s) * patches + b
                    row = p * plan.part_rows + at
                    frame = (f * plan.patch_n + p) * plan.sets + s
                    matrix[1, row, b * plan.time_len + frame] = 1
                    placed = ((f * plan.sets + s) * plan.patch_n + p) * patches + b
                    matrix[2, placed, row] = 1
    return jnp.asarray(matrix, BF16)


def dot(a, b):
    return jnp.dot(a, b, preferred_element_type=F32)


def dot_t(a, b):
    return lax.dot_general(a, b, (((1,), (1,)), ((), ())), preferred_element_type=F32)


def attend_rows(query, key, value, length, heads):
    cols = query.shape[1]
    lane = lax.broadcasted_iota(jnp.int32, (length, cols), 1)
    masks = [(lane >= i * HEAD_WIDTH) & (lane < (i + 1) * HEAD_WIDTH) for i in range(heads)]
    factor = 1.0 / HEAD_WIDTH**0.5
    pieces = []
    for start in range(0, query.shape[0], length):
        q, k, v = (x[start : start + length] for x in (query, key, value))
        spread = jnp.concatenate([jnp.where(m, q, 0.0) for m in masks], axis=0).astype(BF16)
        score = dot_t(spread, k.astype(BF16)) * factor
        score = jnp.exp(score - jnp.max(score, axis=-1, keepdims=True))
        weight = (score / jnp.sum(score, axis=-1, keepdims=True)).astype(BF16)
        mixed = dot(weight, v.astype(BF16))
        total = jnp.zeros((length, cols), F32)
        for i, m in enumerate(masks):
            total = total + jnp.where(m, mixed[i * length : (i + 1) * length], 0.0)
        pieces.append(total)
    return jnp.concatenate(pieces, axis=0) if len(pieces) > 1 else pieces[0]


def normed_slice(slots, own, gain, width):
    center = sum(jnp.sum(s, axis=-1, keepdims=True) for s in slots) * (1.0 / width)
    spread = sum(jnp.sum((s - center) ** 2, axis=-1, keepdims=True) for s in slots) * (1.0 / width)
    return ((own - center) * lax.rsqrt(spread + 1e-06) * gain).astype(BF16)


def block_kernel(
    plan, video_hbm, gain_t_hbm, gain_s_hbm, moves_hbm, wq_t_hbm, wo_t_hbm, wq_s_hbm, wo_s_hbm,
    result, video, gain_t, gain_s, moves, wq_t, wo_t, wq_s, wo_s, staged, gains, vid, base, after, part_t, got_t, part_s, got_s,
    att_t, att_s, pair, proj, proj_all, last, last_all,
    w_sem, vid_sem, got_t_sem, got_s_sem, att_t_sem, att_s_sem, pair_sem, proj_sem, last_sem,
):
    g, f, p, h = (lax.axis_index(a) for a in ("groups", "frame", "patch", "head"))
    fn, pn, hn, depth = plan.frame_n, plan.patch_n, plan.head_n, plan.depth

    def place(df, dp, dh):
        return (g, lax.rem(f + df, fn), lax.rem(p + dp, pn), lax.rem(h + dh, hn))

    loads = [
        pltpu.make_async_copy(src, dst, w_sem.at[i])
        for i, (src, dst) in enumerate(
            (
                (wq_t_hbm, wq_t), (wo_t_hbm, wo_t), (wq_s_hbm, wq_s), (wo_s_hbm, wo_s),
                (video_hbm, video), (gain_t_hbm, gain_t), (gain_s_hbm, gain_s), (moves_hbm, moves),
            )
        )
    ]
    for load in loads[4:] + loads[:4]:
        load.start()

    barrier = pltpu.get_barrier_semaphore()
    offsets = [
        (df, dp, dh)
        for df in range(fn)
        for dp in range(pn)
        for dh in range(hn)
        if df + dp + dh and (dp == 0 or dh == 0)
    ]
    for offset in offsets:
        pl.semaphore_signal(barrier, inc=1, device_id=place(*offset), device_id_type=MESH)

    loads[4].wait()
    for i in range(plan.frames):
        staged[i * plan.patches : (i + 1) * plan.patches] = video[i].astype(F32)
    for j in range(fn):
        lanes = slice(j * depth, (j + 1) * depth)
        vid[f, j] = staged[:, lanes].astype(BF16)
    pl.semaphore_wait(barrier, len(offsets))

    sent = []

    def push(src, dst, sems, number, target):
        copy = pltpu.make_async_remote_copy(
            src_ref=src, dst_ref=dst, send_sem=sems.at[0, number], recv_sem=sems.at[1, number],
            device_id=target, device_id_type=MESH,
        )
        copy.start()
        sent.append(copy)
        return copy

    near = [
        push(vid.at[f], vid.at[f], vid_sem, df, place(df, 0, 0)) for df in range(1, fn)
    ]
    for load in loads[5:]:
        load.wait()
    for j in range(fn):
        lanes = slice(j * depth, (j + 1) * depth)
        gains[0, j] = gain_t[...].reshape(1, plan.width)[:, lanes]
        gains[1, j] = gain_s[...].reshape(1, plan.width)[:, lanes]

    def spread_attention(normed, wq, part, got, got_sem, att, att_sem, length):
        for kind in range(3):
            product = dot(normed, wq[kind])
            for j in range(fn):
                piece = product[j * plan.dest_rows : (j + 1) * plan.dest_rows]
                part[j, kind] = piece.astype(BF16)
        copies = [
            push(part.at[lax.rem(f + df, fn)], got.at[df - 1], got_sem, df, place(df, 0, 0))
            for df in range(1, fn)
        ]
        total = [part[f, kind].astype(F32) for kind in range(3)]
        for df, copy in enumerate(copies):
            copy.wait_recv()
            total = [total[kind] + got[df, kind].astype(F32) for kind in range(3)]
        total = [t.astype(BF16).astype(F32) for t in total]
        att[f] = attend_rows(*total, length, plan.heads).astype(BF16)
        copies = [
            push(att.at[f], att.at[f], att_sem, df, place(df, 0, 0)) for df in range(1, fn)
        ]
        for copy in copies:
            copy.wait_recv()
        return jnp.concatenate([att[j].astype(F32) for j in range(fn)], axis=0).astype(BF16)

    for copy in near:
        copy.wait_recv()

    def series_slot(j):
        return jnp.concatenate([vid[s, j].astype(F32) for s in range(fn)], axis=0)

    normed = normed_slice(
        [series_slot(j) for j in range(fn)], series_slot(f), gains[0, f], plan.width
    )
    normed = dot(moves[0][:, : plan.rows], normed).astype(BF16)
    residual = dot(moves[0][:, : plan.rows], series_slot(f).astype(BF16)).astype(BF16)
    base[...] = dot(moves[1][:, : plan.rows], residual)
    loads[0].wait()
    attended = spread_attention(
        normed, wq_t, part_t, got_t, got_t_sem, att_t, att_t_sem, plan.time_len
    )
    loads[1].wait()
    partial_value = dot_t(attended, wo_t[...]).astype(BF16)
    pair[0] = dot(moves[1][:, : plan.rows], partial_value).astype(BF16)
    copies = [
        push(pair.at[0], pair.at[dh], pair_sem, dh, place(0, 0, dh)) for dh in range(1, hn)
    ]
    total = pair[0].astype(F32)
    for dh, copy in enumerate(copies):
        copy.wait_recv()
        total = total + pair[dh + 1].astype(F32)
    total = (base[...] + total).astype(BF16)
    for q in range(pn):
        proj[q] = total[q * plan.part_rows : (q + 1) * plan.part_rows]
    copies = []
    for dp in range(pn):
        for df in range(fn):
            if df + dp:
                target = place(df, dp, 0)
                number = dp * fn + df
                copies.append(
                    push(proj.at[target[2]], proj_all.at[p, f], proj_sem, number, target)
                )
    proj_all[p, f] = proj[p]
    for copy in copies:
        copy.wait_recv()
    slots = []
    for j in range(fn):
        stacked = jnp.concatenate([proj_all[q, j].astype(F32) for q in range(pn)], axis=0)
        slot = dot(moves[2][:, : plan.rows], stacked.astype(BF16))
        for s in range(fn):
            after[j, s] = slot[s * plan.dest_rows : (s + 1) * plan.dest_rows]
        slots.append(slot)
    own = jnp.concatenate([after[f, s] for s in range(fn)], axis=0)
    normed = normed_slice(slots, own, gains[1, f], plan.width)
    loads[2].wait()
    attended = spread_attention(
        normed, wq_s, part_s, got_s, got_s_sem, att_s, att_s_sem, plan.space_len
    )
    loads[3].wait()
    partial_value = dot_t(attended, wo_s[...])
    for j in range(fn):
        last[j] = partial_value[j * plan.dest_rows : (j + 1) * plan.dest_rows].astype(BF16)
    copies = []
    for dh in range(hn):
        for df in range(fn):
            if df + dh:
                target = place(df, 0, dh)
                number = dh * fn + df
                copies.append(push(last.at[target[1]], last_all.at[h, f], last_sem, number, target))
    last_all[h, f] = last[f]
    for copy in copies:
        copy.wait_recv()
    for j in range(fn):
        total = after[j, f]
        for k in range(hn):
            total = total + last_all[k, j].astype(F32)
        result[:, j * depth : (j + 1) * depth] = total
    for copy in sent:
        copy.wait_send()


def move_tokens(plan, video, gain_time, qkv_time, out_time, gain_space, qkv_space, out_space):
    fn, pn, hn, depth, cols = plan.frame_n, plan.patch_n, plan.head_n, plan.depth, plan.cols
    own, dest, rows = plan.own_rows, plan.dest_rows, plan.rows
    vmem = pl.BlockSpec(memory_space=pltpu.VMEM)
    hbm = pl.BlockSpec(memory_space=pltpu.HBM)
    moves = row_moves(plan)
    pairs = lambda count: pltpu.SemaphoreType.DMA((2, count))
    result = pl.pallas_call(
        functools.partial(block_kernel, plan),
        out_shape=jax.ShapeDtypeStruct((plan.sets * plan.space_len, plan.width), F32),
        in_specs=[hbm] * 8,
        out_specs=vmem,
        scratch_shapes=[
            pltpu.VMEM(video.shape, BF16),
            pltpu.VMEM(gain_time.shape, F32),
            pltpu.VMEM(gain_space.shape, F32),
            pltpu.VMEM(moves.shape, BF16),
            pltpu.VMEM((3, depth, cols), BF16),
            pltpu.VMEM((depth, cols), BF16),
            pltpu.VMEM((3, depth, cols), BF16),
            pltpu.VMEM((depth, cols), BF16),
            pltpu.VMEM((own, plan.width), F32),
            pltpu.VMEM((2, fn, 1, depth), F32),
            pltpu.VMEM((fn, fn, own, depth), BF16),
            pltpu.VMEM((rows, depth), F32),
            pltpu.VMEM((fn, fn, dest, depth), F32),
            pltpu.VMEM((fn, 3, dest, cols), BF16),
            pltpu.VMEM((max(fn - 1, 1), 3, dest, cols), BF16),
            pltpu.VMEM((fn, 3, dest, cols), BF16),
            pltpu.VMEM((max(fn - 1, 1), 3, dest, cols), BF16),
            pltpu.VMEM((fn, dest, cols), BF16),
            pltpu.VMEM((fn, dest, cols), BF16),
            pltpu.VMEM((hn, rows, depth), BF16),
            pltpu.VMEM((pn, plan.part_rows, depth), BF16),
            pltpu.VMEM((pn, fn, plan.part_rows, depth), BF16),
            pltpu.VMEM((fn, dest, depth), BF16),
            pltpu.VMEM((hn, fn, dest, depth), BF16),
            pltpu.SemaphoreType.DMA((8,)),
            pairs(fn),
            pairs(fn),
            pairs(fn),
            pairs(fn),
            pairs(fn),
            pairs(hn),
            pairs(pn * fn),
            pairs(hn * fn),
        ],
        compiler_params=pltpu.CompilerParams(
            collective_id=0, has_side_effects=True, vmem_limit_bytes=63 * 1024 * 1024
        ),
    )(
        video,
        gain_time,
        gain_space,
        moves,
        jnp.transpose(qkv_time, (1, 0, 2)),
        out_time,
        jnp.transpose(qkv_space, (1, 0, 2)),
        out_space,
    )
    return result.reshape(plan.sets, plan.space_len, plan.width)


def solution(mesh):
    placed = (
        P(("groups", "frame"), "patch", None),
        P(),
        P("frame", None, "head"),
        P("frame", "head"),
        P(),
        P("frame", None, "head"),
        P("frame", "head"),
    )

    def on_one(video, gain_time, qkv_time, *others):
        plan = Plan(mesh.shape, video.shape, qkv_time.shape)
        if plan.moves_less():
            return move_tokens(plan, video, gain_time, qkv_time, *others)
        return on_device(video, gain_time, qkv_time, *others)

    return jax.shard_map(
        on_one,
        mesh=mesh,
        in_specs=placed,
        out_specs=P(("groups", "frame", "patch"), None, None),
        check_vma=False,
    )
```

```python
import functools

import jax
import jax.numpy as jnp
import numpy as np
from jax import lax
from jax.experimental import pallas as pl
from jax.experimental.pallas import tpu as pltpu
from jax.sharding import PartitionSpec as P

HEAD_WIDTH = 72


def layer_norm(tokens, gain):
    value_rows = tokens.astype(jnp.float32)
    center = jnp.mean(value_rows, axis=-1, keepdims=True)
    spread = jnp.mean((value_rows - center) ** 2, axis=-1, keepdims=True)
    return ((value_rows - center) * lax.rsqrt(spread + 1e-06) * gain).astype(jnp.bfloat16)


def project_qkv(normed, weight):
    columns = weight.shape[1] * weight.shape[2]
    total = jnp.dot(
        normed, weight.reshape(weight.shape[0], columns), preferred_element_type=jnp.float32
    )
    return total.astype(jnp.bfloat16)


def project_out(attended, weight):
    return lax.dot_general(
        attended, weight, (((1,), (1,)), ((), ())), preferred_element_type=jnp.float32
    )


def attend(qkv, over_first):
    query_rows, key_rows, value_rows = (qkv[:, :, 0], qkv[:, :, 1], qkv[:, :, 2])
    factor = 1.0 / jnp.sqrt(jnp.float32(HEAD_WIDTH))
    if over_first:
        score_matrix = (
            jnp.einsum("abhd,cbhd->bhac", query_rows, key_rows, preferred_element_type=jnp.float32)
            * factor
        )
        attention_weights = jax.nn.softmax(score_matrix, axis=-1).astype(jnp.bfloat16)
        attention_output = jnp.einsum(
            "bhac,cbhd->abhd", attention_weights, value_rows, preferred_element_type=jnp.float32
        )
    else:
        score_matrix = (
            jnp.einsum("abhd,achd->ahbc", query_rows, key_rows, preferred_element_type=jnp.float32)
            * factor
        )
        attention_weights = jax.nn.softmax(score_matrix, axis=-1).astype(jnp.bfloat16)
        attention_output = jnp.einsum(
            "ahbc,achd->abhd", attention_weights, value_rows, preferred_element_type=jnp.float32
        )
    return attention_output.astype(jnp.bfloat16)


def mix_partial(tokens, gain, qkv_weight, out_weight, over_first):
    rows_a, rows_b, width = tokens.shape
    flat = tokens.reshape(rows_a * rows_b, width)
    normed = layer_norm(flat, gain)
    qkv = project_qkv(normed, qkv_weight).reshape(rows_a, rows_b, 3, -1, HEAD_WIDTH)
    attended = attend(qkv, over_first).reshape(rows_a * rows_b, -1)
    partial_value = project_out(attended, out_weight)
    rounded = lax.optimization_barrier(partial_value.astype(jnp.bfloat16)).astype(jnp.float32)
    return (flat, rounded)


def on_device(video, gain_time, qkv_time, out_time, gain_space, qkv_space, out_space):
    frame_size = lax.axis_size("frame")
    patch_size = lax.axis_size("patch")
    device_count = frame_size * patch_size
    series = lax.all_to_all(video, "frame", split_axis=1, concat_axis=0, tiled=True)
    qkv_time, out_time, qkv_space, out_space = (
        lax.all_gather(qkv_time, "frame", axis=0, tiled=True),
        lax.all_gather(out_time, "frame", axis=0, tiled=True),
        lax.all_gather(qkv_space, "frame", axis=0, tiled=True),
        lax.all_gather(out_space, "frame", axis=0, tiled=True),
    )
    frame_count, series_count, width = series.shape
    set_count = frame_count // device_count
    flat, rounded = mix_partial(series, gain_time, qkv_time, out_time, True)
    summed = (
        lax.psum(rounded.astype(jnp.bfloat16), "head")
        .astype(jnp.float32)
        .reshape(device_count, set_count, series_count, width)
    )
    resident = flat.reshape(device_count, set_count, series_count, width)
    after_time = (resident.astype(jnp.float32) + summed).astype(jnp.bfloat16)
    arrived = lax.all_to_all(
        after_time, ("frame", "patch"), split_axis=0, concat_axis=2, tiled=True
    )
    whole_frames = arrived.reshape(set_count, device_count * series_count, width)
    whole_frames = whole_frames.reshape(set_count, frame_size, patch_size, series_count, width)
    whole_frames = jnp.transpose(whole_frames, (0, 2, 1, 3, 4)).reshape(
        set_count, device_count * series_count, width
    )
    flat_space, rounded_space = mix_partial(whole_frames, gain_space, qkv_space, out_space, False)
    summed_space = lax.psum(rounded_space.astype(jnp.bfloat16), "head").astype(jnp.float32)
    result = flat_space.astype(jnp.float32) + summed_space
    return result.reshape(whole_frames.shape)


MESH = pl.DeviceIdType.MESH
BF16 = jnp.bfloat16
F32 = jnp.float32


class Plan:
    def __init__(self, mesh_shape, video, qkv):
        self.frame_n = mesh_shape["frame"]
        self.patch_n = mesh_shape["patch"]
        self.head_n = mesh_shape["head"]
        self.frames, self.patches, self.width = video
        self.depth = qkv[0]
        self.cols = qkv[2]
        self.heads = self.cols // HEAD_WIDTH
        self.time_len = self.frames * self.frame_n
        self.space_len = self.patches * self.patch_n
        self.rows = self.time_len * self.patches
        self.own_rows = self.frames * self.patches
        self.series = self.patches // self.frame_n
        self.sets = self.frames // self.patch_n
        self.part_rows = self.rows // self.patch_n
        self.dest_rows = self.rows // self.frame_n

    def moves_less(self):
        divides = (
            self.patches % self.frame_n == 0
            and self.frames % self.patch_n == 0
            and self.dest_rows % 8 == 0
        )
        tokens = 2 * self.rows * (4 * self.cols + 2 * self.width)
        weights = 2 * (self.frame_n - 1) * self.depth * 4 * self.cols
        return divides and tokens < weights


def row_moves(plan):
    rows, patches = plan.rows, plan.patches
    matrix = np.zeros((3, rows, rows), np.float32)
    for t in range(plan.time_len):
        for b in range(patches):
            matrix[0, b * plan.time_len + t, t * patches + b] = 1
    for f in range(plan.frame_n):
        for p in range(plan.patch_n):
            for s in range(plan.sets):
                for b in range(patches):
                    at = (f * plan.sets + s) * patches + b
                    row = p * plan.part_rows + at
                    frame = (f * plan.patch_n + p) * plan.sets + s
                    matrix[1, row, b * plan.time_len + frame] = 1
                    placed = ((f * plan.sets + s) * plan.patch_n + p) * patches + b
                    matrix[2, placed, row] = 1
    return jnp.asarray(matrix, BF16)


def dot(a, b):
    return jnp.dot(a, b, preferred_element_type=F32)


def dot_t(a, b):
    return lax.dot_general(a, b, (((1,), (1,)), ((), ())), preferred_element_type=F32)


def attend_rows(query, key, value, length, heads):
    cols = query.shape[1]
    lane = lax.broadcasted_iota(jnp.int32, (length, cols), 1)
    masks = [(lane >= i * HEAD_WIDTH) & (lane < (i + 1) * HEAD_WIDTH) for i in range(heads)]
    factor = 1.0 / HEAD_WIDTH**0.5
    pieces = []
    for start in range(0, query.shape[0], length):
        q, k, v = (x[start : start + length] for x in (query, key, value))
        spread = jnp.concatenate([jnp.where(m, q, 0.0) for m in masks], axis=0).astype(BF16)
        score = dot_t(spread, k.astype(BF16)) * factor
        score = jnp.exp(score - jnp.max(score, axis=-1, keepdims=True))
        weight = (score / jnp.sum(score, axis=-1, keepdims=True)).astype(BF16)
        mixed = dot(weight, v.astype(BF16))
        total = jnp.zeros((length, cols), F32)
        for i, m in enumerate(masks):
            total = total + jnp.where(m, mixed[i * length : (i + 1) * length], 0.0)
        pieces.append(total)
    return jnp.concatenate(pieces, axis=0) if len(pieces) > 1 else pieces[0]


def normed_slice(slots, own, gain, width):
    center = sum(jnp.sum(s, axis=-1, keepdims=True) for s in slots) * (1.0 / width)
    spread = sum(jnp.sum((s - center) ** 2, axis=-1, keepdims=True) for s in slots) * (1.0 / width)
    return ((own - center) * lax.rsqrt(spread + 1e-06) * gain).astype(BF16)


def block_kernel(
    plan, video_hbm, gain_t_hbm, gain_s_hbm, moves_hbm, wq_t_hbm, wo_t_hbm, wq_s_hbm, wo_s_hbm,
    result, video, gain_t, gain_s, moves, wq_t, wo_t, wq_s, wo_s, staged, gains, vid_out, vid, base, after, part_t, got_t, part_s, got_s,
    att_t, att_s, pair, proj, proj_all, last, last_all,
    w_sem, vid_sem, got_t_sem, got_s_sem, att_t_sem, att_s_sem, pair_sem, proj_sem, last_sem,
):
    g, f, p, h = (lax.axis_index(a) for a in ("groups", "frame", "patch", "head"))
    fn, pn, hn, depth = plan.frame_n, plan.patch_n, plan.head_n, plan.depth

    def place(df, dp, dh):
        return (g, lax.rem(f + df, fn), lax.rem(p + dp, pn), lax.rem(h + dh, hn))

    loads = [
        pltpu.make_async_copy(src, dst, w_sem.at[i])
        for i, (src, dst) in enumerate(
            (
                (wq_t_hbm, wq_t), (wo_t_hbm, wo_t), (wq_s_hbm, wq_s), (wo_s_hbm, wo_s),
                (video_hbm, video), (gain_t_hbm, gain_t), (gain_s_hbm, gain_s), (moves_hbm, moves),
            )
        )
    ]
    for load in loads[4:] + loads[:4]:
        load.start()

    barrier = pltpu.get_barrier_semaphore()
    offsets = [
        (df, dp, dh)
        for df in range(fn)
        for dp in range(pn)
        for dh in range(hn)
        if df + dp + dh and (dp == 0 or dh == 0)
    ]
    for offset in offsets:
        pl.semaphore_signal(barrier, inc=1, device_id=place(*offset), device_id_type=MESH)

    loads[4].wait()
    for i in range(plan.frames):
        staged[i * plan.patches : (i + 1) * plan.patches] = video[i].astype(F32)
    for load in loads[5:]:
        load.wait()
    tokens = staged[...]
    gain = gain_t[...].reshape(1, plan.width)
    normed = normed_slice([tokens], tokens, gain, plan.width).astype(F32)
    for j in range(fn):
        lanes = slice(j * depth, (j + 1) * depth)
        vid_out[j, 0] = staged[:, lanes].astype(BF16)
        vid_out[j, 1] = normed[:, lanes].astype(BF16)
        gains[0, j] = gain_s[...].reshape(1, plan.width)[:, lanes]
    pl.semaphore_wait(barrier, len(offsets))

    sent = []

    def push(src, dst, sems, number, target):
        copy = pltpu.make_async_remote_copy(
            src_ref=src, dst_ref=dst, send_sem=sems.at[0, number], recv_sem=sems.at[1, number],
            device_id=target, device_id_type=MESH,
        )
        copy.start()
        sent.append(copy)
        return copy

    near = []
    for df in range(1, fn):
        target = place(df, 0, 0)
        near.append(push(vid_out.at[target[1]], vid.at[f], vid_sem, df, target))
    vid[f] = vid_out[f]

    def spread_attention(normed, wq, part, got, got_sem, att, att_sem, length):
        for kind in range(3):
            product = dot(normed, wq[kind])
            for j in range(fn):
                piece = product[j * plan.dest_rows : (j + 1) * plan.dest_rows]
                part[j, kind] = piece.astype(BF16)
        copies = [
            push(part.at[lax.rem(f + df, fn)], got.at[df - 1], got_sem, df, place(df, 0, 0))
            for df in range(1, fn)
        ]
        total = [part[f, kind].astype(F32) for kind in range(3)]
        for df, copy in enumerate(copies):
            copy.wait_recv()
            total = [total[kind] + got[df, kind].astype(F32) for kind in range(3)]
        total = [t.astype(BF16).astype(F32) for t in total]
        att[f] = attend_rows(*total, length, plan.heads).astype(BF16)
        copies = [
            push(att.at[f], att.at[f], att_sem, df, place(df, 0, 0)) for df in range(1, fn)
        ]
        for copy in copies:
            copy.wait_recv()
        return jnp.concatenate([att[j].astype(F32) for j in range(fn)], axis=0).astype(BF16)

    for copy in near:
        copy.wait_recv()

    def series(kind):
        rows = jnp.concatenate([vid[s, kind].astype(F32) for s in range(fn)], axis=0).astype(BF16)
        return dot(moves[0][:, : plan.rows], rows).astype(BF16)

    normed, residual = series(1), series(0)
    base[...] = dot(moves[1][:, : plan.rows], residual)
    loads[0].wait()
    attended = spread_attention(
        normed, wq_t, part_t, got_t, got_t_sem, att_t, att_t_sem, plan.time_len
    )
    loads[1].wait()
    partial_value = dot_t(attended, wo_t[...]).astype(BF16)
    pair[0] = dot(moves[1][:, : plan.rows], partial_value).astype(BF16)
    copies = [
        push(pair.at[0], pair.at[dh], pair_sem, dh, place(0, 0, dh)) for dh in range(1, hn)
    ]
    total = pair[0].astype(F32)
    for dh, copy in enumerate(copies):
        copy.wait_recv()
        total = total + pair[dh + 1].astype(F32)
    total = (base[...] + total).astype(BF16)
    for q in range(pn):
        proj[q] = total[q * plan.part_rows : (q + 1) * plan.part_rows]
    copies = []
    for dp in range(pn):
        for df in range(fn):
            if df + dp:
                target = place(df, dp, 0)
                number = dp * fn + df
                copies.append(
                    push(proj.at[target[2]], proj_all.at[p, f], proj_sem, number, target)
                )
    proj_all[p, f] = proj[p]
    for copy in copies:
        copy.wait_recv()
    slots = []
    for j in range(fn):
        stacked = jnp.concatenate([proj_all[q, j].astype(F32) for q in range(pn)], axis=0)
        slot = dot(moves[2][:, : plan.rows], stacked.astype(BF16))
        for s in range(fn):
            after[j, s] = slot[s * plan.dest_rows : (s + 1) * plan.dest_rows]
        slots.append(slot)
    own = jnp.concatenate([after[f, s] for s in range(fn)], axis=0)
    normed = normed_slice(slots, own, gains[0, f], plan.width)
    loads[2].wait()
    attended = spread_attention(
        normed, wq_s, part_s, got_s, got_s_sem, att_s, att_s_sem, plan.space_len
    )
    loads[3].wait()
    partial_value = dot_t(attended, wo_s[...])
    for j in range(fn):
        last[j] = partial_value[j * plan.dest_rows : (j + 1) * plan.dest_rows].astype(BF16)
    copies = []
    for dh in range(hn):
        for df in range(fn):
            if df + dh:
                target = place(df, 0, dh)
                number = dh * fn + df
                copies.append(push(last.at[target[1]], last_all.at[h, f], last_sem, number, target))
    last_all[h, f] = last[f]
    for copy in copies:
        copy.wait_recv()
    for j in range(fn):
        total = after[j, f]
        for k in range(hn):
            total = total + last_all[k, j].astype(F32)
        result[:, j * depth : (j + 1) * depth] = total
    for copy in sent:
        copy.wait_send()


def move_tokens(plan, video, gain_time, qkv_time, out_time, gain_space, qkv_space, out_space):
    fn, pn, hn, depth, cols = plan.frame_n, plan.patch_n, plan.head_n, plan.depth, plan.cols
    own, dest, rows = plan.own_rows, plan.dest_rows, plan.rows
    vmem = pl.BlockSpec(memory_space=pltpu.VMEM)
    hbm = pl.BlockSpec(memory_space=pltpu.HBM)
    moves = row_moves(plan)
    pairs = lambda count: pltpu.SemaphoreType.DMA((2, count))
    result = pl.pallas_call(
        functools.partial(block_kernel, plan),
        out_shape=jax.ShapeDtypeStruct((plan.sets * plan.space_len, plan.width), F32),
        in_specs=[hbm] * 8,
        out_specs=vmem,
        scratch_shapes=[
            pltpu.VMEM(video.shape, BF16),
            pltpu.VMEM(gain_time.shape, F32),
            pltpu.VMEM(gain_space.shape, F32),
            pltpu.VMEM(moves.shape, BF16),
            pltpu.VMEM((3, depth, cols), BF16),
            pltpu.VMEM((depth, cols), BF16),
            pltpu.VMEM((3, depth, cols), BF16),
            pltpu.VMEM((depth, cols), BF16),
            pltpu.VMEM((own, plan.width), F32),
            pltpu.VMEM((1, fn, 1, depth), F32),
            pltpu.VMEM((fn, 2, own, depth), BF16),
            pltpu.VMEM((fn, 2, own, depth), BF16),
            pltpu.VMEM((rows, depth), F32),
            pltpu.VMEM((fn, fn, dest, depth), F32),
            pltpu.VMEM((fn, 3, dest, cols), BF16),
            pltpu.VMEM((max(fn - 1, 1), 3, dest, cols), BF16),
            pltpu.VMEM((fn, 3, dest, cols), BF16),
            pltpu.VMEM((max(fn - 1, 1), 3, dest, cols), BF16),
            pltpu.VMEM((fn, dest, cols), BF16),
            pltpu.VMEM((fn, dest, cols), BF16),
            pltpu.VMEM((hn, rows, depth), BF16),
            pltpu.VMEM((pn, plan.part_rows, depth), BF16),
            pltpu.VMEM((pn, fn, plan.part_rows, depth), BF16),
            pltpu.VMEM((fn, dest, depth), BF16),
            pltpu.VMEM((hn, fn, dest, depth), BF16),
            pltpu.SemaphoreType.DMA((8,)),
            pairs(fn),
            pairs(fn),
            pairs(fn),
            pairs(fn),
            pairs(fn),
            pairs(hn),
            pairs(pn * fn),
            pairs(hn * fn),
        ],
        compiler_params=pltpu.CompilerParams(
            collective_id=0, has_side_effects=True, vmem_limit_bytes=63 * 1024 * 1024
        ),
    )(
        video,
        gain_time,
        gain_space,
        moves,
        jnp.transpose(qkv_time, (1, 0, 2)),
        out_time,
        jnp.transpose(qkv_space, (1, 0, 2)),
        out_space,
    )
    return result.reshape(plan.sets, plan.space_len, plan.width)


def solution(mesh):
    placed = (
        P(("groups", "frame"), "patch", None),
        P(),
        P("frame", None, "head"),
        P("frame", "head"),
        P(),
        P("frame", None, "head"),
        P("frame", "head"),
    )

    def on_one(video, gain_time, qkv_time, *others):
        plan = Plan(mesh.shape, video.shape, qkv_time.shape)
        if plan.moves_less():
            return move_tokens(plan, video, gain_time, qkv_time, *others)
        return on_device(video, gain_time, qkv_time, *others)

    return jax.shard_map(
        on_one,
        mesh=mesh,
        in_specs=placed,
        out_specs=P(("groups", "frame", "patch"), None, None),
        check_vma=False,
    )
```
